32 devices in a mesh: filt: 4 (over z), space: 8 (over y, x, core).
Axes of the slice: x: 2, y: 2, z: 4, core: 2. Of those that a mesh axis runs over, the one named last changes fastest.
Arguments:
- inputs: bfloat16 [8, 256, 2048], P('space', 'filt'), may hold values from -6 to 6
- weight: bfloat16 [3, 3, 3, 256, 256], P(None, None, None, 'filt'), may hold values from -0.078125 to 0.078125
- bias: bfloat16 [256], P('filt'), may hold values from -4 to 4
- cotangent: bfloat16 [8, 256, 2048], P('space', 'filt'), may hold values from -6 to 6
Outputs:
- output: float32 [8, 256, 2048], P('space', 'filt')
- grad_inputs: float32 [8, 256, 2048], P('space', 'filt')
- grad_weight: float32 [3, 3, 3, 256, 256], P(None, None, None, 'filt')
- grad_bias: float32 [256], P('filt')
The draws below stay inside these ranges and needn't reach their ends.
All inputs are finite; a program needn't handle non-finite values.
Results may differ from the reference program's by a relative error of at most 0.0003.
Values may be sent and summed in bfloat16 or wider, within the bound.
A program may use at most 64 MiB of HBM per device.

```python
import jax
import jax.numpy as jnp
from jax import lax

C = 256
ROWS = 32
WIDE = 64
DEPTH = 8
PLANE = 2048


def block_levels(stream_key, shape, pieces, low, high):
    loudness = 1.0
    for position, blocks in pieces:
        heights = jax.random.uniform(jax.random.fold_in(jax.random.fold_in(stream_key, 6), position), (blocks,), jnp.float32, low / len(pieces), high / len(pieces))
        loudness = loudness * jnp.repeat(jnp.exp(heights), shape[position] // blocks).reshape((-1,) + (1,) * (len(shape) - 1 - position))
    return loudness


def gaussian(key, shape, width, most, pieces=(), kind=jnp.bfloat16):
    values = width * jax.random.normal(key, shape, jnp.float32)
    if pieces:
        values = values * block_levels(key, shape, pieces, -0.22, 0.18)
    return jnp.clip(values, -most, most).astype(kind)


def setup_inputs(seed: int = 0) -> dict:
    streams_of = jax.random.split(jax.random.key(seed), 5)
    inputs = gaussian(streams_of[0], (DEPTH, C, PLANE), 1.0, 6.0, ((0, 8), (1, 4)))
    weight = gaussian(streams_of[1], (3, 3, 3, C, C), (27 * C) ** -0.5, 0.078125, ((3, 4),))
    bias = gaussian(streams_of[2], (C,), 1.0, 4.0, ((0, 4),))
    cotangent = gaussian(streams_of[3], (DEPTH, C, PLANE), 1.0, 6.0, ((0, 8), (1, 4)))
    return dict(inputs=inputs, weight=weight, bias=bias, cotangent=cotangent)


def convolve(volume, kernel):
    result = lax.conv_general_dilated(volume[None], kernel, (1, 1, 1), [(1, 1), (1, 1), (1, 1)], dimension_numbers=('NDCHW', 'DHWIO', 'NDCHW'), precision=lax.Precision.HIGHEST)
    return result[0]

def reference(inputs, weight, bias, cotangent):
    inputs_wide = inputs.astype(jnp.float32).reshape(DEPTH, C, ROWS, WIDE)
    weight_wide = weight.astype(jnp.float32)
    summed, pullback = jax.vjp(convolve, inputs_wide, weight_wide)
    output = summed + bias.astype(jnp.float32)[None, :, None, None]
    grad_wide = cotangent.astype(jnp.float32).reshape(DEPTH, C, ROWS, WIDE)
    grad_in, grad_kernel = pullback(grad_wide)
    factor = 1.0 / jnp.sqrt(jnp.float32(DEPTH * ROWS * WIDE))
    grad_bias = lax.optimization_barrier(jnp.sum(grad_wide, axis=(0, 2, 3))) * factor
    output = output.reshape(DEPTH, C, ROWS * WIDE)
    grad_in = grad_in.reshape(DEPTH, C, ROWS * WIDE)
    return (output, grad_in, grad_kernel * factor, grad_bias)
```

```python
import functools

import jax
import jax.numpy as jnp
from jax import lax
from jax.experimental import pallas as pl
from jax.experimental.pallas import tpu as pltpu
from jax.sharding import PartitionSpec as P

ROWS = 32
WIDE = 64
TILE = 512
BF16 = jnp.bfloat16
F32 = jnp.float32


def remote(src, dst, send_sem, recv_sem, **where):
    return pltpu.make_async_remote_copy(
        src_ref=src,
        dst_ref=dst,
        send_sem=send_sem,
        recv_sem=recv_sem,
        device_id=where,
        device_id_type=pl.DeviceIdType.MESH,
    )


def kernel(
    F, S, Q, factor,
    in_ref, w_ref, bias_ref, cot_ref,
    out_ref, gi_ref, gw_ref, gb_ref,
    xin, xcot, in3, s_cot, s_in, wst, wrx, wf,
    hs_b, hr_b, hs_f, hr_f, grad, gpair, grx, gfin,
    cot_ss, cot_rs, in_ss, in_rs, halo_ss, halo_rs,
    w1_ss, w1_rs, w2_ss, w2_rs,
    hb_ss, hb_rs, hf_ss, hf_rs,
    pair_ss, pair_rs, rs_ss, rs_rs, ag_ss, ag_rs, lo_ss, lo_rs,
):
    f = lax.axis_index("filt")
    s = lax.axis_index("space")
    cf, plane = in_ref.shape
    chans = w_ref.shape[2]
    half = chans // 2
    H = S // 2
    core = lax.rem(s, 2)
    chip = s // 2
    partner = s + 1 - 2 * core
    tiles = plane // TILE

    barrier = pltpu.get_barrier_semaphore()
    for d in range(1, F):
        pl.semaphore_signal(barrier, inc=1, device_id={"filt": lax.rem(f + d, F)},
                            device_id_type=pl.DeviceIdType.MESH)
    for d in range(1, S):
        pl.semaphore_signal(barrier, inc=1, device_id={"space": lax.rem(s + d, S)},
                            device_id_type=pl.DeviceIdType.MESH)
    pl.semaphore_wait(barrier, F - 1 + S - 1)

    def line(own, buf, ss, rs, t, way):
        shard = f - (t - 1) if way == 0 else f + (t - 1)
        src = own if t == 1 else buf.at[shard]
        to = f + 1 if way == 0 else f - 1
        return remote(src, buf.at[shard], ss.at[way, t - 1], rs.at[way, t - 1], filt=to)

    def sends(t, way):
        if way == 0:
            return jnp.logical_and(f - (t - 1) >= 0, f + 1 < F)
        return jnp.logical_and(f + (t - 1) < F, f - 1 >= 0)

    def arrives(t, way):
        return f - t >= 0 if way == 0 else f + t < F

    def start_line(own, buf, ss, rs):
        for way in range(2):
            @pl.when(sends(1, way))
            def _():
                line(own, buf, ss, rs, 1, way).start()

    def relay(own, buf, ss, rs, t):
        for way in range(2):
            @pl.when(arrives(t, way))
            def _():
                shard = f - t if way == 0 else f + t
                remote(own, buf.at[shard], ss.at[way, t - 1], rs.at[way, t - 1],
                       filt=lax.rem(f + 1, F)).wait_recv()
            if t + 1 < F:
                @pl.when(sends(t + 1, way))
                def _():
                    line(own, buf, ss, rs, t + 1, way).start()

    def end_line(own, buf, ss, rs):
        for way in range(2):
            for t in range(1, F):
                @pl.when(sends(t, way))
                def _():
                    line(own, buf, ss, rs, t, way).wait_send()

    lane = lax.broadcasted_iota(jnp.int32, (16, plane), 1)
    col = lax.rem(lane, WIDE)

    def build(src, row0, dst):
        def step(c, _):
            at = pl.multiple_of(c * 16, 16)
            x = src[pl.ds(at, 16), :].astype(F32)
            to = pl.multiple_of(row0 + c * 16, 16)
            for jw in range(3):
                y = x
                if jw == 0:
                    y = jnp.where(col < WIDE - 1, pltpu.roll(x, plane - 1, 1), 0.0)
                if jw == 2:
                    y = jnp.where(col > 0, pltpu.roll(x, 1, 1), 0.0)
                for jr in range(3):
                    z = y
                    if jr == 0:
                        z = jnp.where(lane < plane - WIDE, pltpu.roll(y, plane - WIDE, 1), 0.0)
                    if jr == 2:
                        z = jnp.where(lane >= WIDE, pltpu.roll(y, WIDE, 1), 0.0)
                    dst[jr * 3 + jw, pl.ds(to, 16), :] = z.astype(BF16)
            return 0
        lax.fori_loop(0, cf // 16, step, 0)

    def build_arrived(buf, dst, t):
        for way in range(2):
            @pl.when(arrives(t, way))
            def _():
                shard = f - t if way == 0 else f + t
                build(buf.at[shard], shard * cf, dst)

    def halo(hs, hr, ss, rs, way, n):
        cols = pl.ds(pl.multiple_of(n * TILE, TILE), TILE)
        to = s + 1 if way == 0 else s - 1
        return remote(hs.at[way, :, cols], hr.at[way, :, cols],
                      ss.at[way, n], rs.at[way, n], space=to)

    def convolve(w, src, flip, up, mine, hs, hr, ss, rs):
        def step(n, _):
            cols = pl.ds(pl.multiple_of(n * TILE, TILE), TILE)
            acc = jnp.zeros((3 * cf, TILE), F32)
            for t in range(9):
                wt = jnp.concatenate([w[kd * 9 + t] for kd in range(3)], axis=0)
                acc = acc + jnp.dot(wt, src[8 - t if flip else t, :, cols],
                                    preferred_element_type=F32)
            mine[:, cols] = acc[cf : 2 * cf]
            hs[0, :, cols] = acc[up * cf : (up + 1) * cf]
            hs[1, :, cols] = acc[(2 - up) * cf : (3 - up) * cf]

            @pl.when(s + 1 < S)
            def _():
                halo(hs, hr, ss, rs, 0, n).start()

            @pl.when(s >= 1)
            def _():
                halo(hs, hr, ss, rs, 1, n).start()
            return 0
        lax.fori_loop(0, tiles, step, 0)

    def finish(mine, hs, hr, ss, rs):
        def step(n, _):
            cols = pl.ds(pl.multiple_of(n * TILE, TILE), TILE)

            @pl.when(s >= 1)
            def _():
                halo(hs, hr, ss, rs, 0, n).wait_recv()
                mine[:, cols] += hr[0, :, cols]

            @pl.when(s + 1 < S)
            def _():
                halo(hs, hr, ss, rs, 1, n).wait_recv()
                mine[:, cols] += hr[1, :, cols]

            @pl.when(s + 1 < S)
            def _():
                halo(hs, hr, ss, rs, 0, n).wait_send()

            @pl.when(s >= 1)
            def _():
                halo(hs, hr, ss, rs, 1, n).wait_send()
            return 0
        lax.fori_loop(0, tiles, step, 0)

    start_line(cot_ref, xcot, cot_ss, cot_rs)
    up_halo = remote(in_ref, in3.at[0], halo_ss.at[0], halo_rs.at[0], space=s + 1)
    down_halo = remote(in_ref, in3.at[2], halo_ss.at[1], halo_rs.at[1], space=s - 1)

    @pl.when(s + 1 < S)
    def _():
        up_halo.start()

    @pl.when(s >= 1)
    def _():
        down_halo.start()

    lanes = 128 // cf
    groups = -(-27 // lanes)
    for g in range(groups):
        taps = [min(g + b * groups, 26) for b in range(lanes)]
        x = jnp.concatenate([w_ref[k].astype(F32) for k in taps], axis=0)
        xt = x.T.astype(BF16)
        for to in range(F):
            wst[to, g * cf : (g + 1) * cf, :] = xt[to * cf : (to + 1) * cf]
    wrx[f] = wst[f]
    wrows = groups * cf // Q
    part = lax.rem(s, Q)

    def wpart(ref, shard, q):
        return ref.at[shard, pl.ds(pl.multiple_of(q * wrows, 16), wrows), :]

    def w_first(d):
        to = lax.rem(f + d, F)
        return remote(wpart(wst, to, part), wpart(wrx, f, part), w1_ss.at[d - 1], w1_rs.at[d - 1], filt=to)

    def w_first_in(d):
        frm = lax.rem(f - d + F, F)
        return remote(wpart(wst, frm, part), wpart(wrx, frm, part), w1_ss.at[d - 1], w1_rs.at[d - 1], filt=frm)

    def w_second(d, e):
        frm = lax.rem(f - d + F, F)
        to = (s // Q) * Q + lax.rem(part + e, Q)
        return remote(wpart(wrx, frm, part), wpart(wrx, frm, part),
                      w2_ss.at[d - 1, e - 1], w2_rs.at[d - 1, e - 1], space=to)

    def w_second_in(d, e):
        frm = lax.rem(f - d + F, F)
        q = lax.rem(part - e + Q, Q)
        to = (s // Q) * Q + q
        return remote(wpart(wrx, frm, q), wpart(wrx, frm, q),
                      w2_ss.at[d - 1, e - 1], w2_rs.at[d - 1, e - 1], space=to)

    for d in range(1, F):
        w_first(d).start()

    build(cot_ref, f * cf, s_cot)
    in3[1] = in_ref[...]

    @pl.when(s == 0)
    def _():
        in3[0] = jnp.zeros((cf, plane), BF16)

    @pl.when(s == S - 1)
    def _():
        in3[2] = jnp.zeros((cf, plane), BF16)

    for t in range(1, F):
        relay(cot_ref, xcot, cot_ss, cot_rs, t)
        if t == F - 1:
            start_line(in_ref, xin, in_ss, in_rs)
        build_arrived(xcot, s_cot, t)
        if t == 1:
            for d in range(1, F):
                w_first_in(d).wait_recv()
                for e in range(1, Q):
                    w_second(d, e).start()

    convolve(w_ref, s_cot, False, 2, gi_ref, hs_b, hr_b, hb_ss, hb_rs)
    relay(in_ref, xin, in_ss, in_rs, 1)

    @pl.when(s >= 1)
    def _():
        up_halo.wait_recv()

    @pl.when(s + 1 < S)
    def _():
        down_halo.wait_recv()

    def grads(t, _):
        r = lax.dot_general(in3[...].reshape(3 * cf, plane), s_cot[t], (((1,), (1,)), ((), ())),
                            preferred_element_type=F32)
        for kd in range(3):
            at = pl.multiple_of((kd * 9 + t) * cf, cf)
            for h in range(2):
                grad[h, pl.ds(at, cf), :] = r[kd * cf : (kd + 1) * cf, h * half : (h + 1) * half]
        return 0

    lax.fori_loop(0, 9, grads, 0)
    bsum = jnp.sum(cot_ref[...].astype(F32), axis=1, keepdims=True)
    for h in range(2):
        grad[h, 27 * cf :, :] = jnp.broadcast_to(bsum, (cf, half))
    pair = remote(grad.at[1 - core], gpair, pair_ss, pair_rs, space=partner)
    pair.start()

    build(in_ref, f * cf, s_in)
    build_arrived(xin, s_in, 1)
    for t in range(2, F - 1):
        relay(in_ref, xin, in_ss, in_rs, t)
        if t < F - 2:
            build_arrived(xin, s_in, t)

    pair.wait()
    rows = grad.shape[1]
    chunk = rows // H
    grad[core] += gpair[...]

    def place(ref, h):
        return ref.at[core, pl.ds(pl.multiple_of(h * chunk, 8), chunk), :]

    def scatter(d):
        to = lax.rem(chip + d, H)
        return remote(place(grad, to), grx.at[d - 1], rs_ss.at[d - 1], rs_rs.at[d - 1],
                      space=2 * to + core)

    def spread(d):
        to = lax.rem(chip + d, H)
        return remote(place(gfin, chip), place(gfin, chip), ag_ss.at[d - 1], ag_rs.at[d - 1],
                      space=2 * to + core)

    def spread_in(d):
        frm = lax.rem(chip - d + H, H)
        return remote(place(gfin, frm), place(gfin, frm), ag_ss.at[d - 1], ag_rs.at[d - 1],
                      space=2 * frm + core)

    def local(d):
        frm = lax.rem(chip - d + H, H)
        return remote(place(gfin, frm), place(gfin, frm), lo_ss.at[d], lo_rs.at[d], space=partner)

    def local_in(d):
        frm = lax.rem(chip - d + H, H)
        there = gfin.at[1 - core, pl.ds(pl.multiple_of(frm * chunk, 8), chunk), :]
        return remote(there, there, lo_ss.at[d], lo_rs.at[d], space=partner)

    for d in range(1, H):
        scatter(d).start()

    for d in range(1, F):
        for e in range(1, Q):
            w_second_in(d, e).wait_recv()
    for g in range(groups):
        for b in range(lanes):
            tap = g + b * groups
            if tap < 27:
                wf[tap] = jnp.concatenate(
                    [wrx[k, g * cf : (g + 1) * cf, b * cf : (b + 1) * cf] for k in range(F)], axis=1)
    if F > 3:
        build_arrived(xin, s_in, F - 2)

    for d in range(1, H):
        scatter(d).wait_recv()
    mine_at = pl.ds(pl.multiple_of(chip * chunk, 8), chunk)
    total = grad[core, mine_at, :]
    for d in range(1, H):
        total = total + grx[d - 1]
    gfin[core, mine_at, :] = total * factor
    for d in range(1, H):
        spread(d).start()
    local(0).start()

    relay(in_ref, xin, in_ss, in_rs, F - 1)
    build_arrived(xin, s_in, F - 1)
    convolve(wf, s_in, True, 0, out_ref, hs_f, hr_f, hf_ss, hf_rs)
    finish(gi_ref, hs_b, hr_b, hb_ss, hb_rs)
    for d in range(1, H):
        spread_in(d).wait_recv()
        local(d).start()
    for d in range(H):
        local_in(d).wait_recv()
    for h in range(2):
        gw_ref[:, h * half : (h + 1) * half] = gfin[h, : 27 * cf, :]
    gb_ref[...] = gfin[0, 27 * cf :, :]
    out_ref[...] += bias_ref[...]
    finish(out_ref, hs_f, hr_f, hf_ss, hf_rs)

    end_line(cot_ref, xcot, cot_ss, cot_rs)
    end_line(in_ref, xin, in_ss, in_rs)

    @pl.when(s + 1 < S)
    def _():
        up_halo.wait_send()

    @pl.when(s >= 1)
    def _():
        down_halo.wait_send()

    for d in range(1, F):
        w_first(d).wait_send()
        for e in range(1, Q):
            w_second(d, e).wait_send()
    for d in range(1, H):
        scatter(d).wait_send()
        spread(d).wait_send()
    for d in range(H):
        local(d).wait_send()


def body(F, S, inputs, weight, bias, cotangent):
    planes, cf, plane = inputs.shape
    assert planes == 1
    chans = weight.shape[4]
    H = S // 2
    lanes = 128 // cf
    wrows = -(-27 // lanes) * cf
    Q = S
    while Q > 2 and (wrows % Q or (wrows // Q) % 16):
        Q //= 2
    factor = 1.0 / float(S * plane) ** 0.5
    rows = 28 * cf
    dma = pltpu.SemaphoreType.DMA
    tiles = plane // TILE
    vmem = pl.BlockSpec(memory_space=pltpu.VMEM)
    V = pltpu.VMEM
    out, gi, gw, gb = pl.pallas_call(
        functools.partial(kernel, F, S, Q, factor),
        out_shape=(
            jax.ShapeDtypeStruct((cf, plane), F32),
            jax.ShapeDtypeStruct((cf, plane), F32),
            jax.ShapeDtypeStruct((27 * cf, chans), F32),
            jax.ShapeDtypeStruct((cf, chans // 2), F32),
        ),
        in_specs=[vmem] * 4,
        out_specs=(vmem,) * 4,
        scratch_shapes=[
            V((F, cf, plane), BF16), V((F, cf, plane), BF16), V((3, cf, plane), BF16),
            V((9, chans, plane), BF16), V((9, chans, plane), BF16),
            V((F, wrows, 128), BF16), V((F, wrows, 128), BF16), V((27, cf, chans), BF16),
            V((2, cf, plane), F32), V((2, cf, plane), F32),
            V((2, cf, plane), F32), V((2, cf, plane), F32),
            V((2, rows, chans // 2), F32), V((rows, chans // 2), F32),
            V((H - 1, rows // H, chans // 2), F32), V((2, rows, chans // 2), F32),
            dma((2, F - 1)), dma((2, F - 1)), dma((2, F - 1)), dma((2, F - 1)),
            dma((2,)), dma((2,)),
            dma((F - 1,)), dma((F - 1,)), dma((F - 1, Q - 1)), dma((F - 1, Q - 1)),
            dma((2, tiles)), dma((2, tiles)), dma((2, tiles)), dma((2, tiles)),
            dma, dma, dma((H - 1,)), dma((H - 1,)), dma((H - 1,)), dma((H - 1,)),
            dma((H,)), dma((H,)),
        ],
        compiler_params=pltpu.CompilerParams(
            collective_id=0, has_side_effects=True, vmem_limit_bytes=56 * 1024 * 1024),
        cost_estimate=pl.CostEstimate(
            flops=3 * 2 * 27 * cf * chans * plane, bytes_accessed=8 * 1024 * 1024, transcendentals=0),
    )(
        inputs.reshape(cf, plane),
        weight.reshape(27, cf, chans),
        bias.astype(F32).reshape(cf, 1),
        cotangent.reshape(cf, plane),
    )
    return (
        out.reshape(1, cf, plane),
        gi.reshape(1, cf, plane),
        gw.reshape(3, 3, 3, cf, chans),
        gb[:, 0],
    )


def solution(mesh):
    placed = (
        P("space", "filt", None),
        P(None, None, None, "filt", None),
        P("filt"),
        P("space", "filt", None),
    )
    return jax.shard_map(
        functools.partial(body, mesh.shape["filt"], mesh.shape["space"]),
        mesh=mesh,
        in_specs=placed,
        out_specs=(
            P("space", "filt", None),
            P("space", "filt", None),
            P(None, None, None, "filt", None),
            P("filt"),
        ),
        check_vma=False,
    )
```

```python
import functools

import jax
import jax.numpy as jnp
from jax import lax
from jax.experimental import pallas as pl
from jax.experimental.pallas import tpu as pltpu
from jax.sharding import PartitionSpec as P

ROWS = 32
WIDE = 64
TILE = 512
BF16 = jnp.bfloat16
F32 = jnp.float32


def remote(src, dst, send_sem, recv_sem, **where):
    return pltpu.make_async_remote_copy(
        src_ref=src,
        dst_ref=dst,
        send_sem=send_sem,
        recv_sem=recv_sem,
        device_id=where,
        device_id_type=pl.DeviceIdType.MESH,
    )


def kernel(
    F, S, Q, factor,
    in_ref, w_ref, bias_ref, cot_ref,
    out_ref, gi_ref, gw_ref, gb_ref,
    xin, xcot, in3, s_cot, s_in, wst, wrx, wf,
    hs_b, hr_b, hs_f, hr_f, grad, gpair, grx, gfin,
    cot_ss, cot_rs, in_ss, in_rs, halo_ss, halo_rs,
    w1_ss, w1_rs, w2_ss, w2_rs,
    hb_ss, hb_rs, hf_ss, hf_rs,
    pair_ss, pair_rs, rs_ss, rs_rs, ag_ss, ag_rs, lo_ss, lo_rs,
):
    f = lax.axis_index("filt")
    s = lax.axis_index("space")
    cf, plane = in_ref.shape
    chans = w_ref.shape[2]
    H = S // 2
    core = lax.rem(s, 2)
    chip = s // 2
    partner = s + 1 - 2 * core
    tiles = plane // TILE

    barrier = pltpu.get_barrier_semaphore()
    for d in range(1, F):
        pl.semaphore_signal(barrier, inc=1, device_id={"filt": lax.rem(f + d, F)},
                            device_id_type=pl.DeviceIdType.MESH)
    for d in range(1, S):
        pl.semaphore_signal(barrier, inc=1, device_id={"space": lax.rem(s + d, S)},
                            device_id_type=pl.DeviceIdType.MESH)
    pl.semaphore_wait(barrier, F - 1 + S - 1)

    def line(own, buf, ss, rs, t, way):
        shard = f - (t - 1) if way == 0 else f + (t - 1)
        src = own if t == 1 else buf.at[shard]
        to = f + 1 if way == 0 else f - 1
        return remote(src, buf.at[shard], ss.at[way, t - 1], rs.at[way, t - 1], filt=to)

    def sends(t, way):
        if way == 0:
            return jnp.logical_and(f - (t - 1) >= 0, f + 1 < F)
        return jnp.logical_and(f + (t - 1) < F, f - 1 >= 0)

    def arrives(t, way):
        return f - t >= 0 if way == 0 else f + t < F

    def start_line(own, buf, ss, rs):
        for way in range(2):
            @pl.when(sends(1, way))
            def _():
                line(own, buf, ss, rs, 1, way).start()

    def relay(own, buf, ss, rs, t, follow=False):
        for way in range(2):
            @pl.when(arrives(t, way))
            def _():
                shard = f - t if way == 0 else f + t
                remote(own, buf.at[shard], ss.at[way, t - 1], rs.at[way, t - 1],
                       filt=lax.rem(f + 1, F)).wait_recv()
            if t + 1 < F:
                @pl.when(sends(t + 1, way))
                def _():
                    line(own, buf, ss, rs, t + 1, way).start()
            if follow:
                @pl.when(jnp.logical_and(sends(1, way), t == (f + 1 if way == 0 else F - f)))
                def _():
                    line(in_ref, xin, in_ss, in_rs, 1, way).start()

    def end_line(own, buf, ss, rs):
        for way in range(2):
            for t in range(1, F):
                @pl.when(sends(t, way))
                def _():
                    line(own, buf, ss, rs, t, way).wait_send()

    lane = lax.broadcasted_iota(jnp.int32, (16, plane), 1)
    col = lax.rem(lane, WIDE)

    def build(src, row0, dst):
        def step(c, _):
            at = pl.multiple_of(c * 16, 16)
            x = src[pl.ds(at, 16), :].astype(F32)
            to = pl.multiple_of(row0 + c * 16, 16)
            for jw in range(3):
                y = x
                if jw == 0:
                    y = jnp.where(col < WIDE - 1, pltpu.roll(x, plane - 1, 1), 0.0)
                if jw == 2:
                    y = jnp.where(col > 0, pltpu.roll(x, 1, 1), 0.0)
                for jr in range(3):
                    z = y
                    if jr == 0:
                        z = jnp.where(lane < plane - WIDE, pltpu.roll(y, plane - WIDE, 1), 0.0)
                    if jr == 2:
                        z = jnp.where(lane >= WIDE, pltpu.roll(y, WIDE, 1), 0.0)
                    dst[jr * 3 + jw, pl.ds(to, 16), :] = z.astype(BF16)
            return 0
        lax.fori_loop(0, cf // 16, step, 0)

    def build_arrived(buf, dst, t):
        for way in range(2):
            @pl.when(arrives(t, way))
            def _():
                shard = f - t if way == 0 else f + t
                build(buf.at[shard], shard * cf, dst)

    def halo(hs, hr, ss, rs, way, n):
        cols = pl.ds(pl.multiple_of(n * TILE, TILE), TILE)
        to = s + 1 if way == 0 else s - 1
        return remote(hs.at[way, :, cols], hr.at[way, :, cols],
                      ss.at[way, n], rs.at[way, n], space=to)

    def convolve(w, src, flip, up, mine, hs, hr, ss, rs):
        def step(n, _):
            cols = pl.ds(pl.multiple_of(n * TILE, TILE), TILE)
            acc = jnp.zeros((3 * cf, TILE), F32)
            for t in range(9):
                wt = jnp.concatenate([w[kd * 9 + t] for kd in range(3)], axis=0)
                acc = acc + jnp.dot(wt, src[8 - t if flip else t, :, cols],
                                    preferred_element_type=F32)
            mine[:, cols] = acc[cf : 2 * cf]
            hs[0, :, cols] = acc[up * cf : (up + 1) * cf]
            hs[1, :, cols] = acc[(2 - up) * cf : (3 - up) * cf]

            @pl.when(s + 1 < S)
            def _():
                halo(hs, hr, ss, rs, 0, n).start()

            @pl.when(s >= 1)
            def _():
                halo(hs, hr, ss, rs, 1, n).start()
            return 0
        lax.fori_loop(0, tiles, step, 0)

    def finish(mine, hs, hr, ss, rs):
        def step(n, _):
            cols = pl.ds(pl.multiple_of(n * TILE, TILE), TILE)

            @pl.when(s >= 1)
            def _():
                halo(hs, hr, ss, rs, 0, n).wait_recv()
                mine[:, cols] += hr[0, :, cols]

            @pl.when(s + 1 < S)
            def _():
                halo(hs, hr, ss, rs, 1, n).wait_recv()
                mine[:, cols] += hr[1, :, cols]

            @pl.when(s + 1 < S)
            def _():
                halo(hs, hr, ss, rs, 0, n).wait_send()

            @pl.when(s >= 1)
            def _():
                halo(hs, hr, ss, rs, 1, n).wait_send()
            return 0
        lax.fori_loop(0, tiles, step, 0)

    start_line(cot_ref, xcot, cot_ss, cot_rs)
    up_halo = remote(in_ref, in3.at[0], halo_ss.at[0], halo_rs.at[0], space=s + 1)
    down_halo = remote(in_ref, in3.at[2], halo_ss.at[1], halo_rs.at[1], space=s - 1)

    @pl.when(s + 1 < S)
    def _():
        up_halo.start()

    @pl.when(s >= 1)
    def _():
        down_halo.start()

    lanes = 128 // cf
    groups = -(-27 // lanes)
    for g in range(groups):
        taps = [min(g + b * groups, 26) for b in range(lanes)]
        x = jnp.concatenate([w_ref[k].astype(F32) for k in taps], axis=0)
        xt = x.T.astype(BF16)
        for to in range(F):
            wst[to, g * cf : (g + 1) * cf, :] = xt[to * cf : (to + 1) * cf]
    wrx[f] = wst[f]
    wrows = groups * cf // Q
    part = lax.rem(s, Q)

    def wpart(ref, shard, q):
        return ref.at[shard, pl.ds(pl.multiple_of(q * wrows, 16), wrows), :]

    def w_first(d):
        to = lax.rem(f + d, F)
        return remote(wpart(wst, to, part), wpart(wrx, f, part), w1_ss.at[d - 1], w1_rs.at[d - 1], filt=to)

    def w_first_in(d):
        frm = lax.rem(f - d + F, F)
        return remote(wpart(wst, frm, part), wpart(wrx, frm, part), w1_ss.at[d - 1], w1_rs.at[d - 1], filt=frm)

    def w_second(d, e):
        frm = lax.rem(f - d + F, F)
        to = (s // Q) * Q + lax.rem(part + e, Q)
        return remote(wpart(wrx, frm, part), wpart(wrx, frm, part),
                      w2_ss.at[d - 1, e - 1], w2_rs.at[d - 1, e - 1], space=to)

    def w_second_in(d, e):
        frm = lax.rem(f - d + F, F)
        q = lax.rem(part - e + Q, Q)
        to = (s // Q) * Q + q
        return remote(wpart(wrx, frm, q), wpart(wrx, frm, q),
                      w2_ss.at[d - 1, e - 1], w2_rs.at[d - 1, e - 1], space=to)

    for d in range(1, F):
        w_first(d).start()

    build(cot_ref, f * cf, s_cot)
    in3[1] = in_ref[...]

    @pl.when(s == 0)
    def _():
        in3[0] = jnp.zeros((cf, plane), BF16)

    @pl.when(s == S - 1)
    def _():
        in3[2] = jnp.zeros((cf, plane), BF16)

    stages = chans // 128
    rows = grad.shape[1]
    hrows = rows // 2
    chunk = hrows // H
    per_stage = F // stages
    first = f // per_stage

    def rows_of(c, h):
        return pl.ds(pl.multiple_of(c * hrows + h * chunk, 8), chunk)

    def pair(g):
        there = pl.ds(pl.multiple_of((1 - core) * hrows, 8), hrows)
        return remote(grad.at[g, there, :], gpair.at[g], pair_ss.at[g], pair_rs.at[g], space=partner)

    def scatter(g, d):
        to = lax.rem(chip + d, H)
        return remote(grad.at[g, rows_of(core, to), :], grx.at[g, d - 1],
                      rs_ss.at[g, d - 1], rs_rs.at[g, d - 1], space=2 * to + core)

    def spread(g, d):
        to = lax.rem(chip + d, H)
        mine = gfin.at[g, rows_of(core, chip), :]
        return remote(mine, mine, ag_ss.at[g, d - 1], ag_rs.at[g, d - 1], space=2 * to + core)

    def spread_in(g, d):
        frm = lax.rem(chip - d + H, H)
        there = gfin.at[g, rows_of(core, frm), :]
        return remote(there, there, ag_ss.at[g, d - 1], ag_rs.at[g, d - 1], space=2 * frm + core)

    def local(g, d):
        frm = lax.rem(chip - d + H, H)
        there = gfin.at[g, rows_of(core, frm), :]
        return remote(there, there, lo_ss.at[g, d], lo_rs.at[g, d], space=partner)

    def local_in(g, d):
        frm = lax.rem(chip - d + H, H)
        there = gfin.at[g, rows_of(1 - core, frm), :]
        return remote(there, there, lo_ss.at[g, d], lo_rs.at[g, d], space=partner)

    def grads(g):
        lanes_at = pl.ds(pl.multiple_of(lax.rem(first + g, stages) * 128, 128), 128)

        def step(t, _):
            r = lax.dot_general(in3[...].reshape(3 * cf, plane), s_cot[t, lanes_at, :],
                                (((1,), (1,)), ((), ())), preferred_element_type=F32)
            for kd in range(3):
                at = pl.multiple_of((kd * 9 + t) * cf, cf)
                grad[g, pl.ds(at, cf), :] = r[kd * cf : (kd + 1) * cf]
            return 0

        lax.fori_loop(0, 9, step, 0)
        bsum = jnp.sum(cot_ref[...].astype(F32), axis=1, keepdims=True)
        grad[g, 27 * cf :, :] = jnp.broadcast_to(bsum, (cf, 128))
        pair(g).start()

    def pair_sum(g):
        pair(g).wait()
        here = pl.ds(pl.multiple_of(core * hrows, 8), hrows)
        grad[g, here, :] += gpair[g]
        for d in range(1, H):
            scatter(g, d).start()

    def chunk_sum(g):
        for d in range(1, H):
            scatter(g, d).wait_recv()
        at = rows_of(core, chip)
        total = grad[g, at, :]
        for d in range(1, H):
            total = total + grx[g, d - 1]
        gfin[g, at, :] = total * factor
        for d in range(1, H):
            spread(g, d).start()
        local(g, 0).start()

    def chunks_in(g):
        for d in range(1, H):
            spread_in(g, d).wait_recv()
            local(g, d).start()

    def write_grad(g):
        for d in range(H):
            local_in(g, d).wait_recv()
        lanes_at = pl.ds(pl.multiple_of(lax.rem(first + g, stages) * 128, 128), 128)
        gw_ref[:, lanes_at] = gfin[g, : 27 * cf, :]

    for t in range(1, F):
        relay(cot_ref, xcot, cot_ss, cot_rs, t, True)
        if t == per_stage:
            pair_sum(0)
        if t == F - 1:
            chunk_sum(0)
        build_arrived(xcot, s_cot, t)
        if t == per_stage - 1:
            @pl.when(s >= 1)
            def _():
                up_halo.wait_recv()

            @pl.when(s + 1 < S)
            def _():
                down_halo.wait_recv()

            grads(0)
        if t == 1:
            for d in range(1, F):
                w_first_in(d).wait_recv()
                for e in range(1, Q):
                    w_second(d, e).start()
    for g in range(1, stages):
        grads(g)

    convolve(w_ref, s_cot, False, 2, gi_ref, hs_b, hr_b, hb_ss, hb_rs)
    for g in range(1, stages):
        pair_sum(g)

    relay(in_ref, xin, in_ss, in_rs, 1)
    build(in_ref, f * cf, s_in)
    build_arrived(xin, s_in, 1)
    for t in range(2, F - 1):
        relay(in_ref, xin, in_ss, in_rs, t)
        if t == 2:
            chunks_in(0)
        build_arrived(xin, s_in, t)
    for g in range(1, stages):
        chunk_sum(g)

    for d in range(1, F):
        for e in range(1, Q):
            w_second_in(d, e).wait_recv()
    for g in range(groups):
        for b in range(lanes):
            tap = g + b * groups
            if tap < 27:
                wf[tap] = jnp.concatenate(
                    [wrx[k, g * cf : (g + 1) * cf, b * cf : (b + 1) * cf] for k in range(F)], axis=1)

    relay(in_ref, xin, in_ss, in_rs, F - 1)
    build_arrived(xin, s_in, F - 1)
    convolve(wf, s_in, True, 0, out_ref, hs_f, hr_f, hf_ss, hf_rs)
    for g in range(1, stages):
        chunks_in(g)
    finish(gi_ref, hs_b, hr_b, hb_ss, hb_rs)
    write_grad(0)
    out_ref[...] += jnp.broadcast_to(bias_ref[...].astype(F32), (128, cf)).T[:, :1]
    for g in range(1, stages):
        write_grad(g)
    gb_ref[...] = gfin[0, 27 * cf :, :].T[:1, :]
    finish(out_ref, hs_f, hr_f, hf_ss, hf_rs)

    end_line(cot_ref, xcot, cot_ss, cot_rs)
    end_line(in_ref, xin, in_ss, in_rs)

    @pl.when(s + 1 < S)
    def _():
        up_halo.wait_send()

    @pl.when(s >= 1)
    def _():
        down_halo.wait_send()

    for d in range(1, F):
        w_first(d).wait_send()
        for e in range(1, Q):
            w_second(d, e).wait_send()
    for g in range(stages):
        for d in range(1, H):
            scatter(g, d).wait_send()
            spread(g, d).wait_send()
        for d in range(H):
            local(g, d).wait_send()


def body(F, S, inputs, weight, bias, cotangent):
    planes, cf, plane = inputs.shape
    assert planes == 1
    chans = weight.shape[4]
    H = S // 2
    lanes = 128 // cf
    wrows = -(-27 // lanes) * cf
    Q = 2
    stages = chans // 128
    factor = 1.0 / float(S * plane) ** 0.5
    rows = 28 * cf
    dma = pltpu.SemaphoreType.DMA
    tiles = plane // TILE
    vmem = pl.BlockSpec(memory_space=pltpu.VMEM)
    V = pltpu.VMEM
    out, gi, gw, gb = pl.pallas_call(
        functools.partial(kernel, F, S, Q, factor),
        out_shape=(
            jax.ShapeDtypeStruct((cf, plane), F32),
            jax.ShapeDtypeStruct((cf, plane), F32),
            jax.ShapeDtypeStruct((27 * cf, chans), F32),
            jax.ShapeDtypeStruct((1, cf), F32),
        ),
        in_specs=[vmem] * 4,
        out_specs=(vmem,) * 4,
        scratch_shapes=[
            V((F, cf, plane), BF16), V((F, cf, plane), BF16), V((3, cf, plane), BF16),
            V((9, chans, plane), BF16), V((9, chans, plane), BF16),
            V((F, wrows, 128), BF16), V((F, wrows, 128), BF16), V((27, cf, chans), BF16),
            V((2, cf, plane), F32), V((2, cf, plane), F32),
            V((2, cf, plane), F32), V((2, cf, plane), F32),
            V((stages, rows, 128), F32), V((stages, rows // 2, 128), F32),
            V((stages, H - 1, rows // (2 * H), 128), F32), V((stages, rows, 128), F32),
            dma((2, F - 1)), dma((2, F - 1)), dma((2, F - 1)), dma((2, F - 1)),
            dma((2,)), dma((2,)),
            dma((F - 1,)), dma((F - 1,)), dma((F - 1, Q - 1)), dma((F - 1, Q - 1)),
            dma((2, tiles)), dma((2, tiles)), dma((2, tiles)), dma((2, tiles)),
            dma((stages,)), dma((stages,)), dma((stages, H - 1)), dma((stages, H - 1)),
            dma((stages, H - 1)), dma((stages, H - 1)), dma((stages, H)), dma((stages, H)),
        ],
        compiler_params=pltpu.CompilerParams(
            collective_id=0, has_side_effects=True, vmem_limit_bytes=56 * 1024 * 1024),
        cost_estimate=pl.CostEstimate(
            flops=3 * 2 * 27 * cf * chans * plane, bytes_accessed=8 * 1024 * 1024, transcendentals=0),
    )(
        inputs.reshape(cf, plane),
        weight.reshape(27, cf, chans),
        bias.reshape(1, cf),
        cotangent.reshape(cf, plane),
    )
    return (
        out.reshape(1, cf, plane),
        gi.reshape(1, cf, plane),
        gw.reshape(3, 3, 3, cf, chans),
        gb.reshape(cf),
    )


def solution(mesh):
    placed = (
        P("space", "filt", None),
        P(None, None, None, "filt", None),
        P("filt"),
        P("space", "filt", None),
    )
    return jax.shard_map(
        functools.partial(body, mesh.shape["filt"], mesh.shape["space"]),
        mesh=mesh,
        in_specs=placed,
        out_specs=(
            P("space", "filt", None),
            P("space", "filt", None),
            P(None, None, None, "filt", None),
            P("filt"),
        ),
        check_vma=False,
    )
```

```python
import functools

import jax
import jax.numpy as jnp
from jax import lax
from jax.experimental import pallas as pl
from jax.experimental.pallas import tpu as pltpu
from jax.sharding import PartitionSpec as P

ROWS = 32
WIDE = 64
TILE = 512
BF16 = jnp.bfloat16
F32 = jnp.float32


def remote(src, dst, send_sem, recv_sem, **where):
    return pltpu.make_async_remote_copy(
        src_ref=src,
        dst_ref=dst,
        send_sem=send_sem,
        recv_sem=recv_sem,
        device_id=where,
        device_id_type=pl.DeviceIdType.MESH,
    )


def kernel(
    F, S, Q, factor,
    in_ref, w_ref, bias_ref, cot_ref,
    out_ref, gi_ref, gw_ref, gb_ref,
    xin, xcot, in3, s_cot, s_in, wst, wrx, wf,
    hs_b, hr_b, hs_f, hr_f, grad, gpair, grx, gfin,
    cot_ss, cot_rs, in_ss, in_rs, halo_ss, halo_rs,
    w1_ss, w1_rs, w2_ss, w2_rs,
    hb_ss, hb_rs, hf_ss, hf_rs,
    pair_ss, pair_rs, rs_ss, rs_rs, ag_ss, ag_rs, lo_ss, lo_rs,
):
    f = lax.axis_index("filt")
    s = lax.axis_index("space")
    cf, plane = in_ref.shape
    chans = w_ref.shape[2]
    H = S // 2
    core = lax.rem(s, 2)
    chip = s // 2
    partner = s + 1 - 2 * core
    tiles = plane // TILE

    barrier = pltpu.get_barrier_semaphore()
    for d in range(1, F):
        pl.semaphore_signal(barrier, inc=1, device_id={"filt": lax.rem(f + d, F)},
                            device_id_type=pl.DeviceIdType.MESH)
    for d in range(1, S):
        pl.semaphore_signal(barrier, inc=1, device_id={"space": lax.rem(s + d, S)},
                            device_id_type=pl.DeviceIdType.MESH)
    pl.semaphore_wait(barrier, F - 1 + S - 1)

    def line(own, buf, ss, rs, t, way):
        shard = f - (t - 1) if way == 0 else f + (t - 1)
        src = own if t == 1 else buf.at[shard]
        to = f + 1 if way == 0 else f - 1
        return remote(src, buf.at[shard], ss.at[way, t - 1], rs.at[way, t - 1], filt=to)

    def sends(t, way):
        if way == 0:
            return jnp.logical_and(f - (t - 1) >= 0, f + 1 < F)
        return jnp.logical_and(f + (t - 1) < F, f - 1 >= 0)

    def arrives(t, way):
        return f - t >= 0 if way == 0 else f + t < F

    def start_line(own, buf, ss, rs):
        for way in range(2):
            @pl.when(sends(1, way))
            def _():
                line(own, buf, ss, rs, 1, way).start()

    def relay(own, buf, ss, rs, t, follow=False):
        for way in range(2):
            @pl.when(arrives(t, way))
            def _():
                shard = f - t if way == 0 else f + t
                remote(own, buf.at[shard], ss.at[way, t - 1], rs.at[way, t - 1],
                       filt=lax.rem(f + 1, F)).wait_recv()
            if t + 1 < F:
                @pl.when(sends(t + 1, way))
                def _():
                    line(own, buf, ss, rs, t + 1, way).start()
            if follow:
                @pl.when(jnp.logical_and(sends(1, way), t == (f + 1 if way == 0 else F - f)))
                def _():
                    line(in_ref, xin, in_ss, in_rs, 1, way).start()

    def end_line(own, buf, ss, rs):
        for way in range(2):
            for t in range(1, F):
                @pl.when(sends(t, way))
                def _():
                    line(own, buf, ss, rs, t, way).wait_send()

    lane = lax.broadcasted_iota(jnp.int32, (16, plane), 1)
    col = lax.rem(lane, WIDE)

    def build(src, row0, dst):
        def step(c, _):
            at = pl.multiple_of(c * 16, 16)
            x = src[pl.ds(at, 16), :].astype(F32)
            to = pl.multiple_of(row0 + c * 16, 16)
            for jw in range(3):
                y = x
                if jw == 0:
                    y = jnp.where(col < WIDE - 1, pltpu.roll(x, plane - 1, 1), 0.0)
                if jw == 2:
                    y = jnp.where(col > 0, pltpu.roll(x, 1, 1), 0.0)
                for jr in range(3):
                    z = y
                    if jr == 0:
                        z = jnp.where(lane < plane - WIDE, pltpu.roll(y, plane - WIDE, 1), 0.0)
                    if jr == 2:
                        z = jnp.where(lane >= WIDE, pltpu.roll(y, WIDE, 1), 0.0)
                    dst[jr * 3 + jw, pl.ds(to, 16), :] = z.astype(BF16)
            return 0
        lax.fori_loop(0, cf // 16, step, 0)

    def build_arrived(buf, dst, t):
        for way in range(2):
            @pl.when(arrives(t, way))
            def _():
                shard = f - t if way == 0 else f + t
                build(buf.at[shard], shard * cf, dst)

    def halo(hs, hr, ss, rs, way, n):
        cols = pl.ds(pl.multiple_of(n * TILE, TILE), TILE)
        to = s + 1 if way == 0 else s - 1
        return remote(hs.at[way, :, cols], hr.at[way, :, cols],
                      ss.at[way, n], rs.at[way, n], space=to)

    def convolve(w, src, flip, up, mine, hs, hr, ss, rs):
        def step(n, _):
            cols = pl.ds(pl.multiple_of(n * TILE, TILE), TILE)
            acc = jnp.zeros((3 * cf, TILE), F32)
            for t in range(9):
                wt = jnp.concatenate([w[kd * 9 + t] for kd in range(3)], axis=0)
                acc = acc + jnp.dot(wt, src[8 - t if flip else t, :, cols],
                                    preferred_element_type=F32)
            mine[:, cols] = acc[cf : 2 * cf]
            hs[0, :, cols] = acc[up * cf : (up + 1) * cf]
            hs[1, :, cols] = acc[(2 - up) * cf : (3 - up) * cf]

            @pl.when(s + 1 < S)
            def _():
                halo(hs, hr, ss, rs, 0, n).start()

            @pl.when(s >= 1)
            def _():
                halo(hs, hr, ss, rs, 1, n).start()
            return 0
        lax.fori_loop(0, tiles, step, 0)

    def finish(mine, hs, hr, ss, rs):
        def step(n, _):
            cols = pl.ds(pl.multiple_of(n * TILE, TILE), TILE)

            @pl.when(s >= 1)
            def _():
                halo(hs, hr, ss, rs, 0, n).wait_recv()
                mine[:, cols] += hr[0, :, cols]

            @pl.when(s + 1 < S)
            def _():
                halo(hs, hr, ss, rs, 1, n).wait_recv()
                mine[:, cols] += hr[1, :, cols]

            @pl.when(s + 1 < S)
            def _():
                halo(hs, hr, ss, rs, 0, n).wait_send()

            @pl.when(s >= 1)
            def _():
                halo(hs, hr, ss, rs, 1, n).wait_send()
            return 0
        lax.fori_loop(0, tiles, step, 0)

    start_line(cot_ref, xcot, cot_ss, cot_rs)
    up_halo = remote(in_ref, in3.at[0], halo_ss.at[0], halo_rs.at[0], space=s + 1)
    down_halo = remote(in_ref, in3.at[2], halo_ss.at[1], halo_rs.at[1], space=s - 1)

    @pl.when(s + 1 < S)
    def _():
        up_halo.start()

    @pl.when(s >= 1)
    def _():
        down_halo.start()

    lanes = 128 // cf
    groups = -(-27 // lanes)
    for g in range(groups):
        taps = [min(g + b * groups, 26) for b in range(lanes)]
        x = jnp.concatenate([w_ref[k].astype(F32) for k in taps], axis=0)
        xt = x.T.astype(BF16)
        for to in range(F):
            wst[to, g * cf : (g + 1) * cf, :] = xt[to * cf : (to + 1) * cf]
    wrx[f] = wst[f]
    wrows = groups * cf // Q
    part = lax.rem(s, Q)

    def wpart(ref, shard, q):
        return ref.at[shard, pl.ds(pl.multiple_of(q * wrows, 16), wrows), :]

    def w_first(d):
        to = lax.rem(f + d, F)
        return remote(wpart(wst, to, part), wpart(wrx, f, part), w1_ss.at[d - 1], w1_rs.at[d - 1], filt=to)

    def w_first_in(d):
        frm = lax.rem(f - d + F, F)
        return remote(wpart(wst, frm, part), wpart(wrx, frm, part), w1_ss.at[d - 1], w1_rs.at[d - 1], filt=frm)

    def w_second(d, e):
        frm = lax.rem(f - d + F, F)
        to = (s // Q) * Q + lax.rem(part + e, Q)
        return remote(wpart(wrx, frm, part), wpart(wrx, frm, part),
                      w2_ss.at[d - 1, e - 1], w2_rs.at[d - 1, e - 1], space=to)

    def w_second_in(d, e):
        frm = lax.rem(f - d + F, F)
        q = lax.rem(part - e + Q, Q)
        to = (s // Q) * Q + q
        return remote(wpart(wrx, frm, q), wpart(wrx, frm, q),
                      w2_ss.at[d - 1, e - 1], w2_rs.at[d - 1, e - 1], space=to)

    for d in range(1, F):
        w_first(d).start()

    build(cot_ref, f * cf, s_cot)
    in3[1] = in_ref[...]

    @pl.when(s == 0)
    def _():
        in3[0] = jnp.zeros((cf, plane), BF16)

    @pl.when(s == S - 1)
    def _():
        in3[2] = jnp.zeros((cf, plane), BF16)

    stages = chans // 128
    rows = grad.shape[1]
    hrows = rows // 2
    chunk = hrows // H
    per_stage = F // stages
    first = f // per_stage

    def rows_of(c, h):
        return pl.ds(pl.multiple_of(c * hrows + h * chunk, 8), chunk)

    def pair(g):
        there = pl.ds(pl.multiple_of((1 - core) * hrows, 8), hrows)
        return remote(grad.at[g, there, :], gpair.at[g], pair_ss.at[g], pair_rs.at[g], space=partner)

    def scatter(g, d):
        to = lax.rem(chip + d, H)
        return remote(grad.at[g, rows_of(core, to), :], grx.at[g, d - 1],
                      rs_ss.at[g, d - 1], rs_rs.at[g, d - 1], space=2 * to + core)

    def spread(g, d):
        to = lax.rem(chip + d, H)
        mine = gfin.at[g, rows_of(core, chip), :]
        return remote(mine, mine, ag_ss.at[g, d - 1], ag_rs.at[g, d - 1], space=2 * to + core)

    def spread_in(g, d):
        frm = lax.rem(chip - d + H, H)
        there = gfin.at[g, rows_of(core, frm), :]
        return remote(there, there, ag_ss.at[g, d - 1], ag_rs.at[g, d - 1], space=2 * frm + core)

    def local(g, d):
        frm = lax.rem(chip - d + H, H)
        there = gfin.at[g, rows_of(core, frm), :]
        return remote(there, there, lo_ss.at[g, d], lo_rs.at[g, d], space=partner)

    def local_in(g, d):
        frm = lax.rem(chip - d + H, H)
        there = gfin.at[g, rows_of(1 - core, frm), :]
        return remote(there, there, lo_ss.at[g, d], lo_rs.at[g, d], space=partner)

    def grads(g):
        lanes_at = pl.ds(pl.multiple_of(lax.rem(first + g, stages) * 128, 128), 128)

        def step(t, _):
            r = lax.dot_general(in3[...].reshape(3 * cf, plane), s_cot[t, lanes_at, :],
                                (((1,), (1,)), ((), ())), preferred_element_type=F32)
            for kd in range(3):
                at = pl.multiple_of((kd * 9 + t) * cf, cf)
                grad[g, pl.ds(at, cf), :] = r[kd * cf : (kd + 1) * cf]
            return 0

        lax.fori_loop(0, 9, step, 0)
        bsum = jnp.sum(cot_ref[...].astype(F32), axis=1, keepdims=True)
        grad[g, 27 * cf :, :] = jnp.broadcast_to(bsum, (cf, 128))
        pair(g).start()

    def pair_sum(g):
        pair(g).wait()
        here = pl.ds(pl.multiple_of(core * hrows, 8), hrows)
        grad[g, here, :] += gpair[g]
        for d in range(1, H):
            scatter(g, d).start()

    def chunk_sum(g):
        for d in range(1, H):
            scatter(g, d).wait_recv()
        at = rows_of(core, chip)
        total = grad[g, at, :]
        for d in range(1, H):
            total = total + grx[g, d - 1]
        gfin[g, at, :] = total * factor
        for d in range(1, H):
            spread(g, d).start()
        local(g, 0).start()

    def chunks_in(g):
        for d in range(1, H):
            spread_in(g, d).wait_recv()
            local(g, d).start()

    def write_grad(g):
        for d in range(H):
            local_in(g, d).wait_recv()
        lanes_at = pl.ds(pl.multiple_of(lax.rem(first + g, stages) * 128, 128), 128)
        gw_ref[:, lanes_at] = gfin[g, : 27 * cf, :]

    for t in range(1, F):
        relay(cot_ref, xcot, cot_ss, cot_rs, t, True)
        if t == per_stage:
            pair_sum(0)
        if t == F - 1:
            chunk_sum(0)
        build_arrived(xcot, s_cot, t)
        if t == per_stage - 1:
            @pl.when(s >= 1)
            def _():
                up_halo.wait_recv()

            @pl.when(s + 1 < S)
            def _():
                down_halo.wait_recv()

            grads(0)
        if t == 1:
            for d in range(1, F):
                w_first_in(d).wait_recv()
                for e in range(1, Q):
                    w_second(d, e).start()
    convolve(w_ref, s_cot, False, 2, gi_ref, hs_b, hr_b, hb_ss, hb_rs)
    for g in range(1, stages):
        grads(g)
    relay(in_ref, xin, in_ss, in_rs, 1)
    for g in range(1, stages):
        pair_sum(g)

    build(in_ref, f * cf, s_in)
    build_arrived(xin, s_in, 1)
    for t in range(2, F - 1):
        relay(in_ref, xin, in_ss, in_rs, t)
        if t == 2:
            chunks_in(0)
        build_arrived(xin, s_in, t)
    for g in range(1, stages):
        chunk_sum(g)

    for d in range(1, F):
        for e in range(1, Q):
            w_second_in(d, e).wait_recv()
    for g in range(groups):
        for b in range(lanes):
            tap = g + b * groups
            if tap < 27:
                wf[tap] = jnp.concatenate(
                    [wrx[k, g * cf : (g + 1) * cf, b * cf : (b + 1) * cf] for k in range(F)], axis=1)

    relay(in_ref, xin, in_ss, in_rs, F - 1)
    build_arrived(xin, s_in, F - 1)
    convolve(wf, s_in, True, 0, out_ref, hs_f, hr_f, hf_ss, hf_rs)
    for g in range(1, stages):
        chunks_in(g)
    finish(gi_ref, hs_b, hr_b, hb_ss, hb_rs)
    write_grad(0)
    out_ref[...] += jnp.broadcast_to(bias_ref[...].astype(F32), (128, cf)).T[:, :1]
    for g in range(1, stages):
        write_grad(g)
    gb_ref[...] = gfin[0, 27 * cf :, :].T[:1, :]
    finish(out_ref, hs_f, hr_f, hf_ss, hf_rs)

    end_line(cot_ref, xcot, cot_ss, cot_rs)
    end_line(in_ref, xin, in_ss, in_rs)

    @pl.when(s + 1 < S)
    def _():
        up_halo.wait_send()

    @pl.when(s >= 1)
    def _():
        down_halo.wait_send()

    for d in range(1, F):
        w_first(d).wait_send()
        for e in range(1, Q):
            w_second(d, e).wait_send()
    for g in range(stages):
        for d in range(1, H):
            scatter(g, d).wait_send()
            spread(g, d).wait_send()
        for d in range(H):
            local(g, d).wait_send()


def body(F, S, inputs, weight, bias, cotangent):
    planes, cf, plane = inputs.shape
    assert planes == 1
    chans = weight.shape[4]
    H = S // 2
    lanes = 128 // cf
    wrows = -(-27 // lanes) * cf
    Q = S
    while Q > 2 and (wrows % Q or (wrows // Q) % 16):
        Q //= 2
    stages = chans // 128
    factor = 1.0 / float(S * plane) ** 0.5
    rows = 28 * cf
    dma = pltpu.SemaphoreType.DMA
    tiles = plane // TILE
    vmem = pl.BlockSpec(memory_space=pltpu.VMEM)
    V = pltpu.VMEM
    out, gi, gw, gb = pl.pallas_call(
        functools.partial(kernel, F, S, Q, factor),
        out_shape=(
            jax.ShapeDtypeStruct((cf, plane), F32),
            jax.ShapeDtypeStruct((cf, plane), F32),
            jax.ShapeDtypeStruct((27 * cf, chans), F32),
            jax.ShapeDtypeStruct((1, cf), F32),
        ),
        in_specs=[vmem] * 4,
        out_specs=(vmem,) * 4,
        scratch_shapes=[
            V((F, cf, plane), BF16), V((F, cf, plane), BF16), V((3, cf, plane), BF16),
            V((9, chans, plane), BF16), V((9, chans, plane), BF16),
            V((F, wrows, 128), BF16), V((F, wrows, 128), BF16), V((27, cf, chans), BF16),
            V((2, cf, plane), F32), V((2, cf, plane), F32),
            V((2, cf, plane), F32), V((2, cf, plane), F32),
            V((stages, rows, 128), F32), V((stages, rows // 2, 128), F32),
            V((stages, H - 1, rows // (2 * H), 128), F32), V((stages, rows, 128), F32),
            dma((2, F - 1)), dma((2, F - 1)), dma((2, F - 1)), dma((2, F - 1)),
            dma((2,)), dma((2,)),
            dma((F - 1,)), dma((F - 1,)), dma((F - 1, Q - 1)), dma((F - 1, Q - 1)),
            dma((2, tiles)), dma((2, tiles)), dma((2, tiles)), dma((2, tiles)),
            dma((stages,)), dma((stages,)), dma((stages, H - 1)), dma((stages, H - 1)),
            dma((stages, H - 1)), dma((stages, H - 1)), dma((stages, H)), dma((stages, H)),
        ],
        compiler_params=pltpu.CompilerParams(
            collective_id=0, has_side_effects=True, vmem_limit_bytes=56 * 1024 * 1024),
        cost_estimate=pl.CostEstimate(
            flops=3 * 2 * 27 * cf * chans * plane, bytes_accessed=8 * 1024 * 1024, transcendentals=0),
    )(
        inputs.reshape(cf, plane),
        weight.reshape(27, cf, chans),
        bias.reshape(1, cf),
        cotangent.reshape(cf, plane),
    )
    return (
        out.reshape(1, cf, plane),
        gi.reshape(1, cf, plane),
        gw.reshape(3, 3, 3, cf, chans),
        gb.reshape(cf),
    )


def solution(mesh):
    placed = (
        P("space", "filt", None),
        P(None, None, None, "filt", None),
        P("filt"),
        P("space", "filt", None),
    )
    return jax.shard_map(
        functools.partial(body, mesh.shape["filt"], mesh.shape["space"]),
        mesh=mesh,
        in_specs=placed,
        out_specs=(
            P("space", "filt", None),
            P("space", "filt", None),
            P(None, None, None, "filt", None),
            P("filt"),
        ),
        check_vma=False,
    )
```
